128 devices in a mesh: blk: 8 (over x, core), feat: 16 (over y, z).
Axes of the slice: x: 4, y: 4, z: 4, core: 2. Of those that a mesh axis runs over, the one named last changes fastest.
Arguments:
- features: bfloat16 [128, 131072], P(('blk', 'feat')), may hold values from -24 to 24
- w_self: bfloat16 [128, 256], replicated, may hold values from -0.5 to 0.5
- w_neigh: bfloat16 [128, 256], replicated, may hold values from -0.5 to 0.5
- adjacency_tiles: bfloat16 [1024, 8, 128, 128], P(('blk', 'feat')), as said below
- tile_columns: int32 [1024, 8], P(('blk', 'feat')), may hold values from 0 to 127, as said below
- tile_count: int32 [1024], P(('blk', 'feat')), may hold values from 1 to 8
- cotangent: bfloat16 [131072, 256], P(('blk', 'feat')), may hold values from -0.08984375 to 0.08984375
Outputs:
- hidden_out: bfloat16 [131072, 256], P(('blk', 'feat'))
- grad_self: float32 [128, 256], replicated
- grad_neigh: float32 [128, 256], replicated
The draws below stay inside these ranges and needn't reach their ends.
Inputs may be any that keep to these rules, and one draw needn't show every extreme that they name: `adjacency_tiles`: nonnegative adjacency weights; slots at or beyond tile_count are not used. `tile_columns`: the 8 column blocks of a row block are distinct.
All inputs are finite; a program needn't handle non-finite values.
Results may differ from the reference program's by a relative error of at most 0.0055.
Values may be sent and summed in bfloat16 or wider, within the bound.
No kernel may reach another device: no remote copies, remote signals or barrier semaphores. Data moves between devices by JAX's collectives and lax.ppermute only.
A program may use at most 128 MiB of HBM per device.

```python
import math
import jax
import jax.numpy as jnp
from jax import lax

F = 128
H = 256
BS = 128
TPR = 8
GROUP = 128
NBLK = 1024
NODES = 131072


def draw_adjacency_tiles(key, part):
    key = jax.random.fold_in(key, 11)
    entry_key = jax.random.fold_in(key, 0)
    values = jax.random.uniform(entry_key, (NBLK, TPR, BS, BS), jnp.float32, 0.0, 1.0)
    return (values * (3.0 / math.sqrt(TPR * BS))).astype(jnp.bfloat16)


def draw_tile_columns(key, part):
    key = jax.random.fold_in(key, 12)
    row_keys = jax.random.split(key, NBLK)
    perms = jax.vmap(lambda row_key: jax.random.permutation(row_key, GROUP))(row_keys)
    return perms[:, :TPR].astype(jnp.int32)


def draw_tile_count(key, part):
    key = jax.random.fold_in(key, 13)
    count_key, pick_key = jax.random.split(key)
    drawn_counts = jax.random.randint(count_key, (NBLK,), 1, TPR + 1)
    chosen = jax.random.randint(pick_key, (), 0, NBLK)
    return jnp.where(jnp.arange(NBLK) == chosen, TPR, drawn_counts).astype(jnp.int32)


def with_spikes(entries, stream_key, source, target, shards_of, factor):
    owner, partner = [(jnp.arange(entries.shape[axis_at]) // (entries.shape[axis_at] // shards_of)).reshape([-1 if axis == axis_at else 1 for axis in range(entries.ndim)]) for axis_at in (source, target)]
    chosen = jax.random.permutation(stream_key, shards_of)[partner]
    strong = (owner == chosen) | (owner == (partner + shards_of // 2) % shards_of)
    return jnp.where(strong, factor * entries, entries)


def level_of(key, extent, cuts, low, top_value):
    def one(axis_at, parts):
        heights = jax.random.uniform(jax.random.fold_in(jax.random.fold_in(key, 6), axis_at), (parts,), jnp.float32, low / len(cuts), top_value / len(cuts))
        return jnp.repeat(jnp.exp(heights), extent[axis_at] // parts).reshape((-1,) + (1,) * (len(extent) - axis_at - 1))

    factor_of = one(*cuts[0])
    for cut in cuts[1:]:
        factor_of = factor_of * one(*cut)
    return factor_of


def gaussian(key, shape, spread, limit, cuts=(), held_as=jnp.bfloat16):
    entries = jax.random.normal(key, shape, jnp.float32) * spread
    if len(cuts) > 0:
        entries = level_of(key, shape, cuts, -0.22, 0.18) * entries
    return jnp.clip(entries, min=-limit, max=limit).astype(held_as)


def gaussian_with(rng, shape, width, bound, cuts, heavy, held_as=jnp.bfloat16):
    result = width * jax.random.normal(rng, shape, jnp.float32)
    if cuts:
        result = result * level_of(rng, shape, cuts, -0.22, 0.18)
    return jnp.clip(with_spikes(result, jax.random.fold_in(rng, 3), *heavy), -bound, bound).astype(held_as)


def setup_inputs(seed: int = 0) -> dict:
    key_of = jax.random.split(jax.random.key(seed), 8)
    features = gaussian_with(key_of[0], (F, NODES), 1.0, 24.0, ((0, 128),), (0, 1, 128, 5.5))
    w_self = gaussian(key_of[1], (F, H), F ** -0.5, 0.5)
    w_neigh = gaussian(key_of[2], (F, H), F ** -0.5, 0.5)
    adjacency_tiles = draw_adjacency_tiles(jax.random.fold_in(key_of[7], 71), 0)
    tile_columns = draw_tile_columns(jax.random.fold_in(key_of[7], 71), 0)
    tile_count = draw_tile_count(jax.random.fold_in(key_of[7], 71), 0)
    cotangent = gaussian(key_of[6], (NODES, H), 0.015625, 0.08984375, ((0, 128),))
    return dict(features=features, w_self=w_self, w_neigh=w_neigh, adjacency_tiles=adjacency_tiles, tile_columns=tile_columns, tile_count=tile_count, cotangent=cotangent)


def reference(features, w_self, w_neigh, adjacency_tiles, tile_columns, tile_count, cotangent):
    z_self = jnp.dot(features.T, w_self, preferred_element_type=jnp.float32).astype(jnp.bfloat16)
    z_neigh = jnp.dot(features.T, w_neigh, preferred_element_type=jnp.float32).astype(jnp.bfloat16)
    blocks = z_neigh.reshape(NBLK, BS, H)
    group_start = ((jnp.arange(NBLK) // GROUP) * GROUP).astype(jnp.int32)
    live_tiles = jnp.arange(TPR).astype(jnp.int32)[None, :] < tile_count[:, None]

    def one_block(block_item):
        tile_set, column_set, live_set, group_first = block_item
        picked = blocks[group_first + column_set]
        products = jnp.einsum("tij,tjh->tih", tile_set.astype(jnp.float32), picked.astype(jnp.float32))
        return jnp.sum(jnp.where(live_set[:, None, None], products, 0.0), axis=0)

    aggregated = lax.map(one_block, (adjacency_tiles, tile_columns, live_tiles, group_start)).reshape(NODES, H)
    pre_act = z_self.astype(jnp.float32) + aggregated
    hidden_out = jax.nn.silu(pre_act).astype(jnp.bfloat16)
    sigmoid_pre = jax.nn.sigmoid(pre_act)
    grad_pre = (cotangent.astype(jnp.float32) * sigmoid_pre * (1.0 + pre_act * (1.0 - sigmoid_pre))).astype(jnp.bfloat16)
    grad_blocks = grad_pre.reshape(NBLK, BS, H)

    def spread_block(summed, block_item):
        tile_set, column_set, live_set, group_first, grad_block = block_item
        products = jnp.einsum("tji,jh->tih", tile_set.astype(jnp.float32), grad_block.astype(jnp.float32))
        products = jnp.where(live_set[:, None, None], products, 0.0)
        return summed.at[group_first + column_set].add(products), None

    summed, _ = lax.scan(spread_block, jnp.zeros((NBLK, BS, H), jnp.float32),
                         (adjacency_tiles, tile_columns, live_tiles, group_start, grad_blocks))
    grad_zn = summed.reshape(NODES, H)
    grad_self = jnp.dot(features, grad_pre, preferred_element_type=jnp.float32)
    grad_neigh = jnp.dot(features.astype(jnp.float32), grad_zn, precision=lax.Precision.HIGHEST,
                         preferred_element_type=jnp.float32)
    return (hidden_out, grad_self, grad_neigh)
```

```python
import functools

import jax
import jax.numpy as jnp
from jax import lax
from jax.experimental import pallas as pl
from jax.experimental.pallas import tpu as pltpu
from jax.sharding import PartitionSpec as P

ALL = ("blk", "feat")
CONTRACT_FIRST = (((0,), (0,)), ((), ()))
CONTRACT_LAST = (((1,), (1,)), ((), ()))


def layer_kernel(columns, counts, own, x_ref, tiles_ref, w_ref, cot_ref, hidden_ref, grad_ref):
    blocks, slots, size, _ = tiles_ref.shape
    first = own[0] * (blocks * size)
    w = w_ref[...]
    grad = jnp.zeros(grad_ref.shape, jnp.float32)
    for b in range(blocks):
        gathered = jnp.zeros((x_ref.shape[0], size), jnp.float32)
        for t in range(slots):
            start = pl.multiple_of(columns[b * slots + t] * size, size)
            tile = tiles_ref[b, t]
            tile = jnp.where(t < counts[b], tile, jnp.zeros_like(tile))
            gathered += lax.dot_general(
                x_ref[:, pl.ds(start, size)], tile, CONTRACT_LAST,
                preferred_element_type=jnp.float32,
            )
        own_x = x_ref[:, pl.ds(pl.multiple_of(first + b * size, size), size)]
        both = jnp.concatenate([own_x, gathered.astype(jnp.bfloat16)], axis=0)
        pre = lax.dot_general(both, w, CONTRACT_FIRST, preferred_element_type=jnp.float32)
        s = jax.nn.sigmoid(pre)
        rows = pl.ds(b * size, size)
        hidden_ref[rows, :] = (pre * s).astype(jnp.bfloat16)
        cot = cot_ref[rows, :].astype(jnp.float32)
        grad_pre = (cot * s * (1.0 + pre * (1.0 - s))).astype(jnp.bfloat16)
        grad += jnp.dot(both, grad_pre, preferred_element_type=jnp.float32)
    grad_ref[...] = grad


def per_device(features, w_self, w_neigh, adjacency_tiles, tile_columns, tile_count, cotangent):
    nb, nf = lax.axis_size("blk"), lax.axis_size("feat")
    depth, hidden = w_self.shape
    nodes = cotangent.shape[0]

    def regroup(w):
        return w.reshape(nb, nf, hidden).transpose(1, 0, 2).reshape(depth, hidden)

    w = jnp.concatenate([regroup(w_self), regroup(w_neigh)], axis=0)
    rows = lax.all_to_all(features, "blk", split_axis=1, concat_axis=0, tiled=True)
    x = lax.all_gather(rows, "feat", axis=0, tiled=True)
    own = lax.axis_index("feat").astype(jnp.int32).reshape(1)
    vmem = pl.BlockSpec(memory_space=pltpu.VMEM)
    smem = pl.BlockSpec(memory_space=pltpu.SMEM)
    hidden_out, grad = pl.pallas_call(
        layer_kernel,
        out_shape=(
            jax.ShapeDtypeStruct((nodes, hidden), jnp.bfloat16),
            jax.ShapeDtypeStruct((2 * depth, hidden), jnp.float32),
        ),
        in_specs=[smem, smem, smem, vmem, vmem, vmem, vmem],
        out_specs=(vmem, vmem),
        compiler_params=pltpu.CompilerParams(vmem_limit_bytes=24 * 1024 * 1024),
    )(tile_columns.reshape(-1), tile_count, own, x, adjacency_tiles, w, cotangent)
    parts = grad.reshape(2, depth, hidden).transpose(1, 0, 2)
    parts = lax.all_to_all(parts, ALL, split_axis=0, concat_axis=0, tiled=True)
    mine = jnp.sum(parts, axis=0)
    total = lax.all_to_all(
        jnp.broadcast_to(mine[None], (depth, 2, hidden)), ALL, split_axis=0, concat_axis=0, tiled=True
    )
    total = total.reshape(nf, nb, 2, hidden).transpose(2, 1, 0, 3).reshape(2, depth, hidden)
    return hidden_out, total[0], total[1]


def solution(mesh):
    return jax.shard_map(
        per_device,
        mesh=mesh,
        in_specs=(
            P(ALL, None),
            P(),
            P(),
            P(ALL, None, None, None),
            P(ALL, None),
            P(ALL),
            P(ALL, None),
        ),
        out_specs=(P(ALL, None), P(), P()),
        check_vma=False,
    )
```

```python
import jax
import jax.numpy as jnp
from jax import lax
from jax.experimental import pallas as pl
from jax.experimental.pallas import tpu as pltpu
from jax.sharding import PartitionSpec as P

ALL = ("blk", "feat")
CONTRACT_FIRST = (((0,), (0,)), ((), ()))
CONTRACT_LAST = (((1,), (1,)), ((), ()))
RANGE = range(4)


def device(x, c, y, z):
    return (x * 2 + c) * 16 + y * 4 + z


PLANES = [[device(x, 0, y, z) for x in RANGE for z in RANGE] for y in RANGE]
PLANES += [[device(x, 1, y, z) for x in RANGE for y in RANGE] for z in RANGE]


def ring(step):
    pairs = []
    for x in RANGE:
        for y in RANGE:
            for z in RANGE:
                pairs.append((device(x, 0, y, z), device(x, 0, (y + step) % 4, z)))
                pairs.append((device(x, 1, y, z), device(x, 1, y, (z + step) % 4)))
    return pairs


RIGHT, LEFT = ring(1), ring(-1)
OTHER_CORE = [(d, d ^ 16) for d in range(128)]


def interleave_kernel(core, in_ref, own_ref, other_ref):
    half = own_ref.shape[0]
    step = 16
    for part, out_ref in enumerate((own_ref, other_ref)):
        first = ((core[0] + part) % 2) * half
        for k in range(half // step):
            start = pl.multiple_of(first + k * step, step)
            out_ref[pl.ds(k * step, step)] = jnp.swapaxes(in_ref[:, pl.ds(start, step), :], 0, 1)


def layer_kernel(columns, counts, place, *refs):
    pieces = refs[:8]
    tiles_ref, w_ref, cot_ref, hidden_ref, grad_ref = refs[8:]
    blocks, slots, size, _ = tiles_ref.shape
    chunk = w_ref.shape[2]
    w = jnp.concatenate([w_ref[s, place[1 + k]] for s in range(2) for k in range(8)], axis=0)
    grad = jnp.zeros((16 * chunk, w.shape[1]), jnp.float32)

    def features_of(block):
        return jnp.concatenate([piece[block] for piece in pieces], axis=0)

    for b in range(blocks):
        gathered = jnp.zeros((8 * chunk, size), jnp.float32)
        for t in range(slots):
            tile = tiles_ref[b, t]
            tile = jnp.where(t < counts[b], tile, jnp.zeros_like(tile))
            gathered += lax.dot_general(
                features_of(columns[b * slots + t]), tile, CONTRACT_LAST,
                preferred_element_type=jnp.float32,
            )
        own_x = features_of(place[0] * blocks + b)
        both = jnp.concatenate([own_x, gathered.astype(jnp.bfloat16)], axis=0)
        pre = lax.dot_general(both, w, CONTRACT_FIRST, preferred_element_type=jnp.float32)
        s = jax.nn.sigmoid(pre)
        rows = pl.ds(b * size, size)
        hidden_ref[rows, :] = (pre * s).astype(jnp.bfloat16)
        cot = cot_ref[rows, :].astype(jnp.float32)
        grad_pre = (cot * s * (1.0 + pre * (1.0 - s))).astype(jnp.bfloat16)
        grad += jnp.dot(both, grad_pre, preferred_element_type=jnp.float32)
    for s in range(2):
        for k in range(8):
            start = (s * 8 + k) * chunk
            grad_ref[s, place[1 + k]] = grad[start : start + chunk]


VMEM = pl.BlockSpec(memory_space=pltpu.VMEM)
SMEM = pl.BlockSpec(memory_space=pltpu.SMEM)
PARAMS = pltpu.CompilerParams(vmem_limit_bytes=24 * 1024 * 1024)


def send(array, pairs):
    return lax.ppermute(array, ALL, pairs)


def by_chunk(w):
    w = w.reshape(4, 2, 4, 4, -1)
    w = jnp.stack([w[:, 0].transpose(1, 0, 2, 3), w[:, 1].transpose(2, 0, 1, 3)])
    return w.reshape(8, 16, -1)


def by_row(g):
    g = g.reshape(2, 4, 4, 4, -1)
    g = jnp.stack([g[0].transpose(1, 0, 2, 3), g[1].transpose(1, 2, 0, 3)], axis=1)
    return g.reshape(128, -1)


def per_device(features, w_self, w_neigh, adjacency_tiles, tile_columns, tile_count, cotangent):
    depth, hidden = w_self.shape
    nodes = cotangent.shape[0]
    blocks, slots, size, _ = adjacency_tiles.shape
    core = lax.axis_index("blk") % 2
    feat = lax.axis_index("feat")
    y, z = feat // 4, feat % 4

    out = features.reshape(4, 1, 256, size)
    out = jnp.broadcast_to(out, (4, 4, 256, size)).reshape(16, 256, size)
    rows = lax.all_to_all(
        out, ALL, split_axis=0, concat_axis=0, tiled=True, axis_index_groups=PLANES
    )
    piece = jax.ShapeDtypeStruct((128, 16, size), jnp.bfloat16)
    own, other = pl.pallas_call(
        interleave_kernel,
        out_shape=(piece, piece),
        in_specs=[SMEM, VMEM],
        out_specs=(VMEM, VMEM),
        compiler_params=PARAMS,
    )(core.astype(jnp.int32).reshape(1), rows)

    own_left, other_right = send(own, RIGHT), send(other, LEFT)
    other_left, own_right = send(other, RIGHT), send(own, LEFT)
    own_far, other_far = send(own_left, RIGHT), send(other_right, LEFT)
    swapped = [send(v, OTHER_CORE) for v in (other, other_left, other_right, other_far)]
    pieces = [own, own_left, own_right, own_far, *swapped]

    at = jnp.where(core == 0, y, z)
    partner_at = jnp.where(core == 0, z, y)
    steps = jnp.array([0, 3, 1, 2], jnp.int32)
    place = jnp.concatenate(
        [feat[None], core * 4 + (at + steps) % 4, (1 - core) * 4 + (partner_at + steps) % 4]
    ).astype(jnp.int32)
    w = jnp.stack([by_chunk(w_self), by_chunk(w_neigh)])
    hidden_out, grad = pl.pallas_call(
        layer_kernel,
        out_shape=(
            jax.ShapeDtypeStruct((nodes, hidden), jnp.bfloat16),
            jax.ShapeDtypeStruct((2, 8, 16, hidden), jnp.float32),
        ),
        in_specs=[SMEM, SMEM, SMEM] + [VMEM] * 11,
        out_specs=(VMEM, VMEM),
        compiler_params=PARAMS,
    )(tile_columns.reshape(-1), tile_count, place, *pieces, adjacency_tiles, w, cotangent)
    parts = grad.reshape(2, depth, hidden).transpose(1, 0, 2)
    parts = lax.all_to_all(parts, ALL, split_axis=0, concat_axis=0, tiled=True)
    mine = jnp.sum(parts, axis=0)
    total = lax.all_to_all(
        jnp.broadcast_to(mine[None], (depth, 2, hidden)), ALL, split_axis=0, concat_axis=0, tiled=True
    )
    return hidden_out, by_row(total[:, 0]), by_row(total[:, 1])


def solution(mesh):
    return jax.shard_map(
        per_device,
        mesh=mesh,
        in_specs=(
            P(ALL, None),
            P(),
            P(),
            P(ALL, None, None, None),
            P(ALL, None),
            P(ALL),
            P(ALL, None),
        ),
        out_specs=(P(ALL, None), P(), P()),
        check_vma=False,
    )
```

```python
import jax
import jax.numpy as jnp
from jax import lax
from jax.experimental import pallas as pl
from jax.experimental.pallas import tpu as pltpu
from jax.sharding import PartitionSpec as P

ALL = ("blk", "feat")
CONTRACT_FIRST = (((0,), (0,)), ((), ()))
CONTRACT_LAST = (((1,), (1,)), ((), ()))
RANGE = range(4)


def device(x, c, y, z):
    return (x * 2 + c) * 16 + y * 4 + z


PLANES = [[device(x, 0, y, z) for x in RANGE for z in RANGE] for y in RANGE]
PLANES += [[device(x, 1, y, z) for x in RANGE for y in RANGE] for z in RANGE]


def ring(step, to_other_core=0, other_axis=0):
    pairs = []
    for x in RANGE:
        for c in range(2):
            for y in RANGE:
                for z in RANGE:
                    along_z = c ^ other_axis
                    to_y, to_z = (y, (z + step) % 4) if along_z else ((y + step) % 4, z)
                    pairs.append((device(x, c, y, z), device(x, c ^ to_other_core, to_y, to_z)))
    return pairs


RIGHT, LEFT = ring(1), ring(-1)
RIGHT_ACROSS, LEFT_ACROSS = ring(1, to_other_core=1), ring(-1, to_other_core=1)
LEFT_ON = ring(-1, other_axis=1)
OTHER_CORE = [(d, d ^ 16) for d in range(128)]


def spread_kernel(in_ref, out_ref):
    copies, rows, size = out_ref.shape[1:]
    step = 16
    for k in range(in_ref.shape[1] // (step * size)):
        flat = in_ref[0:1, k * step * size : (k + 1) * step * size]
        block = flat.astype(jnp.float32).reshape(step, size).astype(jnp.bfloat16)
        x, first = divmod(k * step, rows)
        for copy in range(copies):
            out_ref[x, copy, first : first + step] = block


def interleave_kernel(core, in_ref, own_ref, other_ref):
    half = own_ref.shape[0]
    step = 16
    for part, out_ref in enumerate((own_ref, other_ref)):
        first = ((core[0] + part) % 2) * half
        for k in range(half // step):
            start = pl.multiple_of(first + k * step, step)
            out_ref[pl.ds(k * step, step)] = jnp.swapaxes(in_ref[:, pl.ds(start, step), :], 0, 1)


def layer_kernel(columns, counts, place, *refs):
    pieces = refs[:8]
    tiles_ref, w_ref, cot_ref, hidden_ref, grad_ref, both_ref = refs[8:]
    blocks, slots, size, _ = tiles_ref.shape
    chunk = w_ref.shape[2]
    depth = 8 * chunk

    def features_of(block):
        return jnp.concatenate([piece[block] for piece in pieces], axis=0)

    for b in range(blocks):
        nodes = slice(b * size, (b + 1) * size)
        both_ref[:depth, nodes] = features_of(place[0] * blocks + b)
        x = jnp.concatenate([features_of(columns[b * slots + t]) for t in range(slots)], axis=1)
        tiles = []
        for t in range(slots):
            tile = tiles_ref[b, t]
            tiles.append(jnp.where(t < counts[b], tile, jnp.zeros_like(tile)))
        gathered = lax.dot_general(
            x, jnp.concatenate(tiles, axis=1), CONTRACT_LAST, preferred_element_type=jnp.float32
        )
        both_ref[depth:, nodes] = gathered.astype(jnp.bfloat16)
    w = jnp.concatenate([w_ref[s, place[1 + k]] for s in range(2) for k in range(8)], axis=0)
    both = both_ref[...]
    pre = lax.dot_general(both, w, CONTRACT_FIRST, preferred_element_type=jnp.float32)
    s = jax.nn.sigmoid(pre)
    hidden = pre * s
    hidden_ref[...] = hidden.astype(jnp.bfloat16)
    grad_pre = (cot_ref[...].astype(jnp.float32) * (s + hidden * (1.0 - s))).astype(jnp.bfloat16)
    grad = jnp.dot(both, grad_pre, preferred_element_type=jnp.float32)
    for k in range(8):
        first, stride = place[9 + k], place[17 + k // 4]
        for i in range(chunk):
            row = first + (i // 4) * 32 + (i % 4) * stride
            for s in range(2):
                at = s * depth + k * chunk + i
                grad_ref[row, s : s + 1] = grad[at : at + 1]


VMEM = pl.BlockSpec(memory_space=pltpu.VMEM)
SMEM = pl.BlockSpec(memory_space=pltpu.SMEM)
PARAMS = pltpu.CompilerParams(vmem_limit_bytes=24 * 1024 * 1024)


def send(array, pairs):
    return lax.ppermute(array, ALL, pairs)


def by_chunk(w):
    w = w.reshape(4, 2, 4, 4, -1)
    w = jnp.stack([w[:, 0].transpose(1, 0, 2, 3), w[:, 1].transpose(2, 0, 1, 3)])
    return w.reshape(8, 16, -1)


def per_device(features, w_self, w_neigh, adjacency_tiles, tile_columns, tile_count, cotangent):
    depth, hidden = w_self.shape
    nodes = cotangent.shape[0]
    blocks, slots, size, _ = adjacency_tiles.shape
    core = lax.axis_index("blk") % 2
    feat = lax.axis_index("feat")
    y, z = feat // 4, feat % 4

    out = pl.pallas_call(
        spread_kernel,
        out_shape=jax.ShapeDtypeStruct((4, 4, 256, size), jnp.bfloat16),
        in_specs=[VMEM],
        out_specs=VMEM,
        compiler_params=PARAMS,
    )(features).reshape(16, 256, size)
    rows = lax.all_to_all(
        out, ALL, split_axis=0, concat_axis=0, tiled=True, axis_index_groups=PLANES
    )
    piece = jax.ShapeDtypeStruct((128, 16, size), jnp.bfloat16)
    own, other = pl.pallas_call(
        interleave_kernel,
        out_shape=(piece, piece),
        in_specs=[SMEM, VMEM],
        out_specs=(VMEM, VMEM),
        compiler_params=PARAMS,
    )(core.astype(jnp.int32).reshape(1), rows)

    own_left, across_right = send(own, RIGHT), send(other, LEFT_ACROSS)
    across_left, own_right = send(other, RIGHT_ACROSS), send(own, LEFT)
    own_far, across_far = send(own_left, RIGHT), send(across_right, LEFT_ON)
    across = send(other, OTHER_CORE)
    pieces = [own, own_left, own_right, own_far, across, across_left, across_right, across_far]

    steps = jnp.array([0, 3, 1, 2], jnp.int32)
    at = (jnp.where(core == 0, y, z) + steps) % 4
    partner_at = (jnp.where(core == 0, z, y) + steps) % 4
    cores = jnp.stack([core, 1 - core])
    chunks = (cores[:, None] * 4 + jnp.stack([at, partner_at])).reshape(-1)
    strides = jnp.where(cores == 0, 1, 4)
    first_rows = cores[:, None] * 16 + jnp.stack([at, partner_at]) * (4 // strides)[:, None]
    place = jnp.concatenate([feat[None], chunks, first_rows.reshape(-1), strides]).astype(jnp.int32)
    w = jnp.stack([by_chunk(w_self), by_chunk(w_neigh)])
    hidden_out, grad = pl.pallas_call(
        layer_kernel,
        out_shape=(
            jax.ShapeDtypeStruct((nodes, hidden), jnp.bfloat16),
            jax.ShapeDtypeStruct((depth, 2, hidden), jnp.float32),
        ),
        in_specs=[SMEM, SMEM, SMEM] + [VMEM] * 11,
        out_specs=(VMEM, VMEM),
        scratch_shapes=[pltpu.VMEM((2 * depth, nodes), jnp.bfloat16)],
        compiler_params=PARAMS,
    )(tile_columns.reshape(-1), tile_count, place, *pieces, adjacency_tiles, w, cotangent)
    parts = lax.all_to_all(grad, ALL, split_axis=0, concat_axis=0, tiled=True)
    mine = jnp.sum(parts, axis=0)
    total = lax.all_to_all(
        jnp.broadcast_to(mine[None], (depth, 2, hidden)), ALL, split_axis=0, concat_axis=0, tiled=True
    )
    return hidden_out, total[:, 0], total[:, 1]


def solution(mesh):
    return jax.shard_map(
        per_device,
        mesh=mesh,
        in_specs=(
            P(ALL, None),
            P(),
            P(),
            P(ALL, None, None, None),
            P(ALL, None),
            P(ALL),
            P(ALL, None),
        ),
        out_specs=(P(ALL, None), P(), P()),
        check_vma=False,
    )
```

```python
import jax
import jax.numpy as jnp
from jax import lax
from jax.experimental import pallas as pl
from jax.experimental.pallas import tpu as pltpu
from jax.sharding import PartitionSpec as P

ALL = ("blk", "feat")
CONTRACT_FIRST = (((0,), (0,)), ((), ()))
CONTRACT_LAST = (((1,), (1,)), ((), ()))
RANGE = range(4)


def device(x, c, y, z):
    return (x * 2 + c) * 16 + y * 4 + z


PLANES = [[device(x, 0, y, z) for x in RANGE for z in RANGE] for y in RANGE]
PLANES += [[device(x, 1, y, z) for x in RANGE for y in RANGE] for z in RANGE]


def ring(step, to_other_core=0):
    pairs = []
    for x in RANGE:
        for y in RANGE:
            for z in RANGE:
                pairs.append((device(x, 0, y, z), device(x, to_other_core, (y + step) % 4, z)))
                pairs.append((device(x, 1, y, z), device(x, 1 - to_other_core, y, (z + step) % 4)))
    return pairs


RIGHT, LEFT, FAR = ring(1), ring(-1), ring(2)
RIGHT_ACROSS, LEFT_ACROSS, FAR_ACROSS = ring(1, 1), ring(-1, 1), ring(2, 1)
OTHER_CORE = [(d, d ^ 16) for d in range(128)]


def spread_kernel(in_ref, out_ref):
    copies, rows, size = out_ref.shape[1:]
    step = 16
    for k in range(in_ref.shape[1] // (step * size)):
        flat = in_ref[0:1, k * step * size : (k + 1) * step * size]
        block = flat.astype(jnp.float32).reshape(step, size).astype(jnp.bfloat16)
        x, first = divmod(k * step, rows)
        for copy in range(copies):
            out_ref[x, copy, first : first + step] = block


def arrange_kernel(place, w_self_ref, w_neigh_ref, out_ref, wide_ref, placed_ref):
    depth = w_self_ref.shape[0]
    wide_ref[:depth] = w_self_ref[...].astype(jnp.float32)
    wide_ref[depth:] = w_neigh_ref[...].astype(jnp.float32)
    for at, row in feature_rows(place):
        for s in range(2):
            placed_ref[s * depth + at : s * depth + at + 1] = wide_ref[pl.ds(s * depth + row, 1)]
    out_ref[...] = placed_ref[...].astype(jnp.bfloat16)


def feature_rows(place):
    for k in range(8):
        first, stride = place[k], place[8 + k // 4]
        for i in range(16):
            yield k * 16 + i, first + (i // 4) * 32 + (i % 4) * stride


def select_kernel(meta, lists, in_ref, w_ref, *refs):
    out_refs, rows_ref, built_ref, sems = refs[:8], *refs[8:]
    half = rows_ref.shape[0] // 2
    step = 16
    blocks, slots = lists.shape[2:]
    copies = []
    for part in range(2):
        first = ((meta[0] + part) % 2) * half
        for k in range(half // step):
            start = pl.multiple_of(first + k * step, step)
            rows_ref[pl.ds(part * half + k * step, step)] = jnp.swapaxes(
                in_ref[:, pl.ds(start, step), :], 0, 1
            )
    for place in (3, 1, 2, 0):
        for part in range(2):
            m = 2 * place + part
            for b in range(blocks):
                for t in range(slots):
                    block = lists[place, part, b, t]
                    built_ref[m, b * slots + t] = rows_ref[part * half + block]
                own = meta[1 + place] * blocks + b
                built_ref[m, blocks * slots + b] = rows_ref[part * half + own]
            copy = pltpu.make_async_copy(built_ref.at[m], out_refs[m], sems.at[m])
            copy.start()
            copies.append(copy)
    for copy in copies:
        copy.wait()


def aggregate_kernel(counts, *refs):
    pieces = refs[:8]
    tiles_ref, both_ref = refs[8:]
    blocks, slots, size, _ = tiles_ref.shape
    depth = both_ref.shape[0] // 2

    def features_of(k):
        return jnp.concatenate([piece[k] for piece in pieces], axis=0)

    for b in range(blocks):
        nodes = slice(b * size, (b + 1) * size)
        both_ref[:depth, nodes] = features_of(blocks * slots + b)
        x = jnp.concatenate([features_of(b * slots + t) for t in range(slots)], axis=1)
        tiles = []
        for t in range(slots):
            tile = tiles_ref[b, t]
            tiles.append(jnp.where(t < counts[b], tile, jnp.zeros_like(tile)))
        gathered = lax.dot_general(
            x, jnp.concatenate(tiles, axis=1), CONTRACT_LAST, preferred_element_type=jnp.float32
        )
        both_ref[depth:, nodes] = gathered.astype(jnp.bfloat16)


def layer_kernel(place, both_ref, w_ref, cot_ref, hidden_ref, grad_ref):
    depth = both_ref.shape[0] // 2
    both = both_ref[...]
    pre = lax.dot_general(both, w_ref[...], CONTRACT_FIRST, preferred_element_type=jnp.float32)
    s = jax.nn.sigmoid(pre)
    hidden = pre * s
    hidden_ref[...] = hidden.astype(jnp.bfloat16)
    grad_pre = (cot_ref[...].astype(jnp.float32) * (s + hidden * (1.0 - s))).astype(jnp.bfloat16)
    grad = jnp.dot(both, grad_pre, preferred_element_type=jnp.float32)
    for at, row in feature_rows(place):
        for s in range(2):
            grad_ref[row, s : s + 1] = grad[s * depth + at : s * depth + at + 1]


VMEM = pl.BlockSpec(memory_space=pltpu.VMEM)
SMEM = pl.BlockSpec(memory_space=pltpu.SMEM)
HBM = pl.BlockSpec(memory_space=pltpu.HBM)
ANY = pl.BlockSpec(memory_space=pl.ANY)
PARAMS = pltpu.CompilerParams(vmem_limit_bytes=24 * 1024 * 1024)


def send(array, pairs):
    return lax.ppermute(array, ALL, pairs)


def per_device(features, w_self, w_neigh, adjacency_tiles, tile_columns, tile_count, cotangent):
    depth, hidden = w_self.shape
    nodes = cotangent.shape[0]
    blocks, slots, size, _ = adjacency_tiles.shape
    core = lax.axis_index("blk") % 2
    feat = lax.axis_index("feat")
    y, z = feat // 4, feat % 4

    out = pl.pallas_call(
        spread_kernel,
        out_shape=jax.ShapeDtypeStruct((4, 4, 256, size), jnp.bfloat16),
        in_specs=[VMEM],
        out_specs=VMEM,
        compiler_params=PARAMS,
    )(features).reshape(16, 256, size)
    rows = lax.all_to_all(
        out, ALL, split_axis=0, concat_axis=0, tiled=True, axis_index_groups=PLANES
    )
    steps = jnp.array([0, 3, 1, 2], jnp.int32)
    at = (jnp.where(core == 0, y, z) + steps) % 4
    partner_at = (jnp.where(core == 0, z, y) + jnp.array([2, 3, 1, 0], jnp.int32)) % 4
    chip = jnp.where(core == 0, at * 4 + z, y * 4 + at)
    meta = jnp.concatenate([core[None], chip]).astype(jnp.int32)
    cores = jnp.stack([core, 1 - core])
    strides = jnp.where(cores == 0, 1, 4)
    first_rows = cores[:, None] * 16 + jnp.stack([at, partner_at]) * (4 // strides)[:, None]
    place = jnp.concatenate([first_rows.reshape(-1), strides]).astype(jnp.int32)
    w = pl.pallas_call(
        arrange_kernel,
        out_shape=jax.ShapeDtypeStruct((2 * depth, hidden), jnp.bfloat16),
        in_specs=[SMEM, VMEM, VMEM],
        out_specs=VMEM,
        scratch_shapes=[pltpu.VMEM((2 * depth, hidden), jnp.float32)] * 2,
        compiler_params=PARAMS,
    )(place, w_self, w_neigh)

    here = jnp.stack([tile_columns, send(tile_columns, OTHER_CORE)])
    lists = jnp.stack([here, send(here, RIGHT), send(here, LEFT), send(here, FAR)])
    listed = blocks * slots + blocks
    piece = jax.ShapeDtypeStruct((listed, 16, size), jnp.bfloat16)
    own, across, own_l, across_l, own_r, across_r, own_f, across_f = pl.pallas_call(
        select_kernel,
        out_shape=(piece,) * 8,
        in_specs=[SMEM, SMEM, VMEM, ANY],
        out_specs=(HBM,) * 8,
        scratch_shapes=[
            pltpu.VMEM((256, 16, size), jnp.bfloat16),
            pltpu.VMEM((8, listed, 16, size), jnp.bfloat16),
            pltpu.SemaphoreType.DMA((8,)),
        ],
        compiler_params=PARAMS,
    )(meta, lists, rows, w)
    pieces = [own, send(own_r, RIGHT), send(own_l, LEFT), send(own_f, FAR)]
    pieces += [send(across_f, FAR_ACROSS), send(across_r, RIGHT_ACROSS), send(across_l, LEFT_ACROSS)]
    pieces += [send(across, OTHER_CORE)]

    both = pl.pallas_call(
        aggregate_kernel,
        out_shape=jax.ShapeDtypeStruct((2 * depth, nodes), jnp.bfloat16),
        in_specs=[SMEM] + [VMEM] * 9,
        out_specs=VMEM,
        compiler_params=PARAMS,
    )(tile_count, *pieces, adjacency_tiles)
    hidden_out, grad = pl.pallas_call(
        layer_kernel,
        out_shape=(
            jax.ShapeDtypeStruct((nodes, hidden), jnp.bfloat16),
            jax.ShapeDtypeStruct((depth, 2, hidden), jnp.float32),
        ),
        in_specs=[SMEM] + [VMEM] * 3,
        out_specs=(VMEM, VMEM),
        compiler_params=PARAMS,
    )(place, both, w, cotangent)
    parts = lax.all_to_all(grad, ALL, split_axis=0, concat_axis=0, tiled=True)
    mine = jnp.sum(parts, axis=0).astype(jnp.bfloat16)
    total = lax.all_to_all(
        jnp.broadcast_to(mine[None], (depth, 2, hidden)), ALL, split_axis=0, concat_axis=0, tiled=True
    )
    total = total.astype(jnp.float32)
    return hidden_out, total[:, 0], total[:, 1]


def solution(mesh):
    return jax.shard_map(
        per_device,
        mesh=mesh,
        in_specs=(
            P(ALL, None),
            P(),
            P(),
            P(ALL, None, None, None),
            P(ALL, None),
            P(ALL),
            P(ALL, None),
        ),
        out_specs=(P(ALL, None), P(), P()),
        check_vma=False,
    )
```

```python
import jax
import jax.numpy as jnp
from jax import lax
from jax.experimental import pallas as pl
from jax.experimental.pallas import tpu as pltpu
from jax.sharding import PartitionSpec as P

ALL = ("blk", "feat")
CONTRACT_FIRST = (((0,), (0,)), ((), ()))
CONTRACT_LAST = (((1,), (1,)), ((), ()))
RANGE = range(4)


def device(x, c, y, z):
    return (x * 2 + c) * 16 + y * 4 + z


PLANES = [[device(x, 0, y, z) for x in RANGE for z in RANGE] for y in RANGE]
PLANES += [[device(x, 1, y, z) for x in RANGE for y in RANGE] for z in RANGE]


def ring(step, to_other_core=0):
    pairs = []
    for x in RANGE:
        for y in RANGE:
            for z in RANGE:
                pairs.append((device(x, 0, y, z), device(x, to_other_core, (y + step) % 4, z)))
                pairs.append((device(x, 1, y, z), device(x, 1 - to_other_core, y, (z + step) % 4)))
    return pairs


RIGHT, LEFT, FAR = ring(1), ring(-1), ring(2)
RIGHT_ACROSS, LEFT_ACROSS, FAR_ACROSS = ring(1, 1), ring(-1, 1), ring(2, 1)
OTHER_CORE = [(d, d ^ 16) for d in range(128)]


def spread_kernel(in_ref, out_ref):
    copies, rows, size = out_ref.shape[1:]
    step = 16
    for k in range(in_ref.shape[1] // (step * size)):
        flat = in_ref[0:1, k * step * size : (k + 1) * step * size]
        block = flat.astype(jnp.float32).reshape(step, size).astype(jnp.bfloat16)
        x, first = divmod(k * step, rows)
        for copy in range(copies):
            out_ref[x, copy, first : first + step] = block


def arrange_kernel(place, w_self_ref, w_neigh_ref, columns_ref, out_ref, columns_out_ref, wide_ref, placed_ref):
    columns_out_ref[...] = columns_ref[...]
    depth = w_self_ref.shape[0]
    wide_ref[:depth] = w_self_ref[...].astype(jnp.float32)
    wide_ref[depth:] = w_neigh_ref[...].astype(jnp.float32)
    for s, at, row in feature_rows(place):
        placed_ref[at : at + 1] = wide_ref[pl.ds(s * depth + row, 1)]
    out_ref[...] = placed_ref[...].astype(jnp.bfloat16)


def feature_rows(place):
    for k in range(8):
        first, stride = place[k], place[8 + k]
        for i in range(16):
            at = k // 4 * 128 + k % 4 * 16 + i
            row = first + (i // 4) * 32 + (i % 4) * stride
            yield 0, at, row
            yield 1, at + 64, row


def interleave_kernel(meta, lists, in_ref, w_ref, rows_ref, *out_refs):
    half = rows_ref.shape[0] // 2
    step = 16
    for part in range(2):
        first = ((meta[0] + part) % 2) * half
        for k in range(half // step):
            start = pl.multiple_of(first + k * step, step)
            rows_ref[pl.ds(part * half + k * step, step)] = jnp.swapaxes(
                in_ref[:, pl.ds(start, step), :], 0, 1
            )
    select(meta, lists, rows_ref, out_refs, EARLY)


def select_kernel(meta, lists, rows_ref, *out_refs):
    select(meta, lists, rows_ref, out_refs, LATE)


def select(meta, lists, rows_ref, out_refs, messages):
    half = rows_ref.shape[0] // 2
    blocks, slots = lists.shape[2:]
    for (place, part), out_ref in zip(messages, out_refs):
        for b in range(blocks):
            for t in range(slots):
                out_ref[b * slots + t] = rows_ref[part * half + lists[place, part, b, t]]
            out_ref[blocks * slots + b] = rows_ref[part * half + meta[1 + place] * blocks + b]


EARLY = ((2, 0), (1, 0))
LATE = ((0, 1), (3, 0), (3, 1), (2, 1), (1, 1), (0, 0))


def aggregate(counts, pieces, tiles_ref, both_ref):
    blocks, slots, size, _ = tiles_ref.shape
    depth = both_ref.shape[0] // 2

    def features_of(k):
        return jnp.concatenate([piece[k] for piece in pieces], axis=0)

    for b in range(blocks):
        nodes = slice(b * size, (b + 1) * size)
        both_ref[:depth, nodes] = features_of(blocks * slots + b)
        x = jnp.concatenate([features_of(b * slots + t) for t in range(slots)], axis=1)
        tiles = []
        for t in range(slots):
            tile = tiles_ref[b, t]
            tiles.append(jnp.where(t < counts[b], tile, jnp.zeros_like(tile)))
        gathered = lax.dot_general(
            x, jnp.concatenate(tiles, axis=1), CONTRACT_LAST, preferred_element_type=jnp.float32
        )
        both_ref[depth:, nodes] = gathered.astype(jnp.bfloat16)


def first_half_kernel(counts, *refs):
    tiles_ref, w_ref, both_ref, pre_ref = refs[4:]
    aggregate(counts, refs[:4], tiles_ref, both_ref)
    pre_ref[...] = lax.dot_general(
        both_ref[...], w_ref[:128], CONTRACT_FIRST, preferred_element_type=jnp.float32
    )


def second_half_kernel(counts, place, *refs):
    tiles_ref, w_ref, first_ref, pre_ref, cot_ref, hidden_ref, grad_ref, both_ref = refs[4:]
    aggregate(counts, refs[:4], tiles_ref, both_ref)
    pre = pre_ref[...] + lax.dot_general(
        both_ref[...], w_ref[128:], CONTRACT_FIRST, preferred_element_type=jnp.float32
    )
    s = jax.nn.sigmoid(pre)
    hidden = pre * s
    hidden_ref[...] = hidden.astype(jnp.bfloat16)
    grad_pre = (cot_ref[...].astype(jnp.float32) * (s + hidden * (1.0 - s))).astype(jnp.bfloat16)
    both = jnp.concatenate([first_ref[...], both_ref[...]], axis=0)
    grad = jnp.dot(both, grad_pre, preferred_element_type=jnp.float32)
    for s, at, row in feature_rows(place):
        grad_ref[row, s : s + 1] = grad[at : at + 1]


def finish_kernel(total_ref, grad_self_ref, grad_neigh_ref):
    grad_self_ref[...] = total_ref[:, 0, :].astype(jnp.float32)
    grad_neigh_ref[...] = total_ref[:, 1, :].astype(jnp.float32)


VMEM = pl.BlockSpec(memory_space=pltpu.VMEM)
SMEM = pl.BlockSpec(memory_space=pltpu.SMEM)
HBM = pl.BlockSpec(memory_space=pltpu.HBM)
ANY = pl.BlockSpec(memory_space=pl.ANY)
PARAMS = pltpu.CompilerParams(vmem_limit_bytes=24 * 1024 * 1024)


def send(array, pairs):
    return lax.ppermute(array, ALL, pairs)


def per_device(features, w_self, w_neigh, adjacency_tiles, tile_columns, tile_count, cotangent):
    depth, hidden = w_self.shape
    nodes = cotangent.shape[0]
    blocks, slots, size, _ = adjacency_tiles.shape
    core = lax.axis_index("blk") % 2
    feat = lax.axis_index("feat")
    y, z = feat // 4, feat % 4

    out = pl.pallas_call(
        spread_kernel,
        out_shape=jax.ShapeDtypeStruct((4, 4, 256, size), jnp.bfloat16),
        in_specs=[VMEM],
        out_specs=VMEM,
        compiler_params=PARAMS,
    )(features).reshape(16, 256, size)
    rows = lax.all_to_all(
        out, ALL, split_axis=0, concat_axis=0, tiled=True, axis_index_groups=PLANES
    )
    steps = jnp.array([0, 3, 1, 2], jnp.int32)
    ring_at = jnp.where(core == 0, y, z) + steps
    chip = jnp.where(core == 0, ring_at % 4 * 4 + z, y * 4 + ring_at % 4)
    meta = jnp.concatenate([core[None], chip]).astype(jnp.int32)
    piece_core = jnp.array([0, 0, 0, 1, 0, 1, 1, 1], jnp.int32) ^ core
    piece_at = jnp.where(piece_core == 0, y, z) + jnp.array([0, 3, 1, 0, 2, 2, 3, 1], jnp.int32)
    strides = jnp.where(piece_core == 0, 1, 4)
    first_rows = piece_core * 16 + piece_at % 4 * jnp.where(piece_core == 0, 4, 1)
    place = jnp.concatenate([first_rows, strides]).astype(jnp.int32)
    w, columns = pl.pallas_call(
        arrange_kernel,
        out_shape=(
            jax.ShapeDtypeStruct((2 * depth, hidden), jnp.bfloat16),
            jax.ShapeDtypeStruct(tile_columns.shape, tile_columns.dtype),
        ),
        in_specs=[SMEM, VMEM, VMEM, VMEM],
        out_specs=(VMEM, VMEM),
        scratch_shapes=[pltpu.VMEM((2 * depth, hidden), jnp.float32)] * 2,
        compiler_params=PARAMS,
    )(place, w_self, w_neigh, tile_columns)

    here = jnp.stack([columns, send(columns, OTHER_CORE)])
    lists = jnp.stack([here, send(here, RIGHT), send(here, LEFT), send(here, FAR)])
    listed = blocks * slots + blocks
    piece = jax.ShapeDtypeStruct((listed, 16, size), jnp.bfloat16)
    rows, own_r, own_l = pl.pallas_call(
        interleave_kernel,
        out_shape=(jax.ShapeDtypeStruct((256, 16, size), jnp.bfloat16), piece, piece),
        in_specs=[SMEM, SMEM, VMEM, ANY],
        out_specs=(VMEM,) * 3,
        compiler_params=PARAMS,
    )(meta, lists, rows, w)
    across, own_f, across_f, across_r, across_l, own = pl.pallas_call(
        select_kernel,
        out_shape=(piece,) * 6,
        in_specs=[SMEM, SMEM, VMEM],
        out_specs=(VMEM,) * 6,
        compiler_params=PARAMS,
    )(meta, lists, rows)
    first = [own, send(own_r, RIGHT), send(own_l, LEFT), send(across, OTHER_CORE)]
    second = [send(own_f, FAR), send(across_f, FAR_ACROSS)]
    second += [send(across_r, RIGHT_ACROSS), send(across_l, LEFT_ACROSS)]

    both = jax.ShapeDtypeStruct((depth, nodes), jnp.bfloat16)
    first_both, first_pre = pl.pallas_call(
        first_half_kernel,
        out_shape=(both, jax.ShapeDtypeStruct((nodes, hidden), jnp.float32)),
        in_specs=[SMEM] + [VMEM] * 6,
        out_specs=(VMEM, VMEM),
        compiler_params=PARAMS,
    )(tile_count, *first, adjacency_tiles, w)
    hidden_out, grad = pl.pallas_call(
        second_half_kernel,
        out_shape=(
            jax.ShapeDtypeStruct((nodes, hidden), jnp.bfloat16),
            jax.ShapeDtypeStruct((depth, 2, hidden), jnp.float32),
        ),
        in_specs=[SMEM, SMEM] + [VMEM] * 9,
        out_specs=(VMEM, VMEM),
        scratch_shapes=[pltpu.VMEM(both.shape, both.dtype)],
        compiler_params=PARAMS,
    )(tile_count, place, *second, adjacency_tiles, w, first_both, first_pre, cotangent)
    parts = lax.all_to_all(grad, ALL, split_axis=0, concat_axis=0, tiled=True)
    mine = jnp.sum(parts, axis=0).astype(jnp.bfloat16)
    total = lax.all_to_all(
        jnp.broadcast_to(mine[None], (depth, 2, hidden)), ALL, split_axis=0, concat_axis=0, tiled=True
    )
    summed = jax.ShapeDtypeStruct((depth, hidden), jnp.float32)
    grad_self, grad_neigh = pl.pallas_call(
        finish_kernel,
        out_shape=(summed, summed),
        in_specs=[VMEM],
        out_specs=(VMEM, VMEM),
        compiler_params=PARAMS,
    )(total)
    return hidden_out, grad_self, grad_neigh


def solution(mesh):
    return jax.shard_map(
        per_device,
        mesh=mesh,
        in_specs=(
            P(ALL, None),
            P(),
            P(),
            P(ALL, None, None, None),
            P(ALL, None),
            P(ALL),
            P(ALL, None),
        ),
        out_specs=(P(ALL, None), P(), P()),
        check_vma=False,
    )
```

```python
import jax
import jax.numpy as jnp
from jax import lax
from jax.experimental import pallas as pl
from jax.experimental.pallas import tpu as pltpu
from jax.sharding import PartitionSpec as P

ALL = ("blk", "feat")
CONTRACT_FIRST = (((0,), (0,)), ((), ()))
CONTRACT_LAST = (((1,), (1,)), ((), ()))
RANGE = range(4)


def device(x, c, y, z):
    return (x * 2 + c) * 16 + y * 4 + z


PLANES = [[device(x, 0, y, z) for x in RANGE for z in RANGE] for y in RANGE]
PLANES += [[device(x, 1, y, z) for x in RANGE for y in RANGE] for z in RANGE]


def ring(step, to_other_core=0):
    pairs = []
    for x in RANGE:
        for y in RANGE:
            for z in RANGE:
                pairs.append((device(x, 0, y, z), device(x, to_other_core, (y + step) % 4, z)))
                pairs.append((device(x, 1, y, z), device(x, 1 - to_other_core, y, (z + step) % 4)))
    return pairs


RIGHT, LEFT, FAR = ring(1), ring(-1), ring(2)
RIGHT_ACROSS, LEFT_ACROSS, FAR_ACROSS = ring(1, 1), ring(-1, 1), ring(2, 1)
OTHER_CORE = [(d, d ^ 16) for d in range(128)]


def spread_kernel(in_ref, out_ref):
    copies, rows, size = out_ref.shape[1:]
    step = 16
    for k in range(in_ref.shape[1] // (step * size)):
        flat = in_ref[0:1, k * step * size : (k + 1) * step * size]
        block = flat.astype(jnp.float32).reshape(step, size).astype(jnp.bfloat16)
        x, first = divmod(k * step, rows)
        for copy in range(copies):
            out_ref[x, copy, first : first + step] = block


def turn_kernel(counts, tiles_ref, turned_ref):
    blocks, slots, size, _ = tiles_ref.shape
    for b in range(blocks):
        for t in range(slots):
            tile = tiles_ref[b, t]
            tile = jnp.where(t < counts[b], tile, jnp.zeros_like(tile))
            turned_ref[b, t * size : (t + 1) * size] = tile.T


def arrange_kernel(place, w_self_ref, w_neigh_ref, columns_ref, out_ref, columns_out_ref, wide_ref, placed_ref):
    columns_out_ref[...] = columns_ref[...]
    depth = w_self_ref.shape[0]
    wide_ref[:depth] = w_self_ref[...].astype(jnp.float32)
    wide_ref[depth:] = w_neigh_ref[...].astype(jnp.float32)
    for s, at, row in feature_rows(place):
        placed_ref[at : at + 1] = wide_ref[pl.ds(s * depth + row, 1)]
    out_ref[...] = placed_ref[...].astype(jnp.bfloat16)


def feature_rows(place):
    for k in range(8):
        first, stride = place[k], place[8 + k]
        for i in range(16):
            at = k // 4 * 128 + k % 4 * 16 + i
            row = first + (i // 4) * 32 + (i % 4) * stride
            yield 0, at, row
            yield 1, at + 64, row


def select_kernel(meta, lists, in_ref, w_ref, turned_ref, *refs):
    out_refs, rows_ref = refs[:-1], refs[-1]
    half = rows_ref.shape[0] // 2
    step = 16
    for part in range(2):
        first = ((meta[0] + part) % 2) * half
        for k in range(half // step):
            start = pl.multiple_of(first + k * step, step)
            rows_ref[pl.ds(part * half + k * step, step)] = jnp.swapaxes(
                in_ref[:, pl.ds(start, step), :], 0, 1
            )
    blocks, slots = lists.shape[2:]
    listed = blocks * slots
    for (place, part), out_ref in zip(MESSAGES, out_refs):
        for b in range(blocks):
            for t in range(slots):
                out_ref[b * slots + t] = rows_ref[part * half + lists[place, part, b, t]]
            out_ref[listed + b] = rows_ref[part * half + meta[1 + place] * blocks + b]


MESSAGES = ((2, 0), (1, 0), (0, 1), (3, 0), (3, 1), (2, 1), (1, 1), (0, 0))


def aggregate(pieces, turned_ref, both_ref):
    blocks, width, size = turned_ref.shape
    slots = width // size
    depth = both_ref.shape[0] // 2

    def features_of(k):
        return jnp.concatenate([piece[k] for piece in pieces], axis=0)

    for b in range(blocks):
        nodes = slice(b * size, (b + 1) * size)
        both_ref[:depth, nodes] = features_of(blocks * slots + b)
        x = jnp.concatenate([features_of(b * slots + t) for t in range(slots)], axis=1)
        gathered = jnp.dot(x, turned_ref[b], preferred_element_type=jnp.float32)
        both_ref[depth:, nodes] = gathered.astype(jnp.bfloat16)


def first_half_kernel(*refs):
    tiles_ref, w_ref, both_ref, pre_ref = refs[4:]
    aggregate(refs[:4], tiles_ref, both_ref)
    pre_ref[...] = lax.dot_general(
        both_ref[...], w_ref[:128], CONTRACT_FIRST, preferred_element_type=jnp.float32
    )


def second_half_kernel(place, *refs):
    tiles_ref, w_ref, first_ref, pre_ref, cot_ref, hidden_hbm, grad_ref, both_ref, hidden_ref, sems = refs[4:]
    aggregate(refs[:4], tiles_ref, both_ref)
    nodes = both_ref.shape[1]
    step = nodes // sems.shape[0]
    grad = jnp.zeros((2 * both_ref.shape[0], grad_ref.shape[2]), jnp.float32)
    stores = []
    for k in range(sems.shape[0]):
        rows = pl.ds(k * step, step)
        both = jnp.concatenate([first_ref[:, rows], both_ref[:, rows]], axis=0)
        pre = pre_ref[rows, :] + lax.dot_general(
            both_ref[:, rows], w_ref[128:], CONTRACT_FIRST, preferred_element_type=jnp.float32
        )
        s = jax.nn.sigmoid(pre)
        hidden = pre * s
        hidden_ref[rows, :] = hidden.astype(jnp.bfloat16)
        stores.append(pltpu.make_async_copy(hidden_ref.at[rows, :], hidden_hbm.at[rows, :], sems.at[k]))
        stores[-1].start()
        slope = s + hidden * (1.0 - s)
        grad_pre = (cot_ref[rows, :].astype(jnp.float32) * slope).astype(jnp.bfloat16)
        grad += jnp.dot(both, grad_pre, preferred_element_type=jnp.float32)
    for s, at, row in feature_rows(place):
        grad_ref[row, s : s + 1] = grad[at : at + 1]
    for store in stores:
        store.wait()


def finish_kernel(total_ref, grad_self_ref, grad_neigh_ref):
    grad_self_ref[...] = total_ref[:, 0, :].astype(jnp.float32)
    grad_neigh_ref[...] = total_ref[:, 1, :].astype(jnp.float32)


VMEM = pl.BlockSpec(memory_space=pltpu.VMEM)
SMEM = pl.BlockSpec(memory_space=pltpu.SMEM)
HBM = pl.BlockSpec(memory_space=pltpu.HBM)
ANY = pl.BlockSpec(memory_space=pl.ANY)
PARAMS = pltpu.CompilerParams(vmem_limit_bytes=24 * 1024 * 1024)


def send(array, pairs):
    return lax.ppermute(array, ALL, pairs)


def per_device(features, w_self, w_neigh, adjacency_tiles, tile_columns, tile_count, cotangent):
    depth, hidden = w_self.shape
    nodes = cotangent.shape[0]
    blocks, slots, size, _ = adjacency_tiles.shape
    core = lax.axis_index("blk") % 2
    feat = lax.axis_index("feat")
    y, z = feat // 4, feat % 4

    out = pl.pallas_call(
        spread_kernel,
        out_shape=jax.ShapeDtypeStruct((4, 4, 256, size), jnp.bfloat16),
        in_specs=[VMEM],
        out_specs=VMEM,
        compiler_params=PARAMS,
    )(features).reshape(16, 256, size)
    rows = lax.all_to_all(
        out, ALL, split_axis=0, concat_axis=0, tiled=True, axis_index_groups=PLANES
    )
    steps = jnp.array([0, 3, 1, 2], jnp.int32)
    ring_at = jnp.where(core == 0, y, z) + steps
    chip = jnp.where(core == 0, ring_at % 4 * 4 + z, y * 4 + ring_at % 4)
    meta = jnp.concatenate([core[None], chip]).astype(jnp.int32)
    piece_core = jnp.array([0, 0, 0, 1, 0, 1, 1, 1], jnp.int32) ^ core
    piece_at = jnp.where(piece_core == 0, y, z) + jnp.array([0, 3, 1, 3, 2, 2, 1, 0], jnp.int32)
    strides = jnp.where(piece_core == 0, 1, 4)
    first_rows = piece_core * 16 + piece_at % 4 * jnp.where(piece_core == 0, 4, 1)
    place = jnp.concatenate([first_rows, strides]).astype(jnp.int32)
    turned = pl.pallas_call(
        turn_kernel,
        out_shape=jax.ShapeDtypeStruct((blocks, slots * size, size), jnp.bfloat16),
        in_specs=[SMEM, VMEM],
        out_specs=VMEM,
        compiler_params=PARAMS,
    )(tile_count, adjacency_tiles)
    w, columns = pl.pallas_call(
        arrange_kernel,
        out_shape=(
            jax.ShapeDtypeStruct((2 * depth, hidden), jnp.bfloat16),
            jax.ShapeDtypeStruct(tile_columns.shape, tile_columns.dtype),
        ),
        in_specs=[SMEM, VMEM, VMEM, VMEM],
        out_specs=(VMEM, VMEM),
        scratch_shapes=[pltpu.VMEM((2 * depth, hidden), jnp.float32)] * 2,
        compiler_params=PARAMS,
    )(place, w_self, w_neigh, tile_columns)

    here = jnp.stack([columns, send(columns, OTHER_CORE)])
    lists = jnp.stack([here, send(here, RIGHT), send(here, LEFT), send(here, FAR)])
    listed = blocks * slots + blocks
    piece = jax.ShapeDtypeStruct((listed, 16, size), jnp.bfloat16)
    own_r, own_l, across, own_f, across_f, across_r, across_l, own = pl.pallas_call(
        select_kernel,
        out_shape=(piece,) * 8,
        in_specs=[SMEM, SMEM, VMEM, ANY, ANY],
        out_specs=(VMEM,) * 8,
        scratch_shapes=[pltpu.VMEM((256, 16, size), jnp.bfloat16)],
        compiler_params=PARAMS,
    )(meta, lists, rows, w, turned)
    first = [own, send(own_r, RIGHT)]
    first += [send(own_l, LEFT), send(across_r, RIGHT_ACROSS)]
    second = [send(own_f, FAR), send(across_f, FAR_ACROSS)]
    second += [send(across_l, LEFT_ACROSS), send(across, OTHER_CORE)]

    both = jax.ShapeDtypeStruct((depth, nodes), jnp.bfloat16)
    first_both, first_pre = pl.pallas_call(
        first_half_kernel,
        out_shape=(both, jax.ShapeDtypeStruct((nodes, hidden), jnp.float32)),
        in_specs=[VMEM] * 6,
        out_specs=(VMEM, VMEM),
        compiler_params=PARAMS,
    )(*first, turned, w)
    hidden_out, grad = pl.pallas_call(
        second_half_kernel,
        out_shape=(
            jax.ShapeDtypeStruct((nodes, hidden), jnp.bfloat16),
            jax.ShapeDtypeStruct((depth, 2, hidden), jnp.float32),
        ),
        in_specs=[SMEM] + [VMEM] * 9,
        out_specs=(ANY, VMEM),
        scratch_shapes=[
            pltpu.VMEM(both.shape, both.dtype),
            pltpu.VMEM((nodes, hidden), jnp.bfloat16),
            pltpu.SemaphoreType.DMA((2,)),
        ],
        compiler_params=PARAMS,
    )(place, *second, turned, w, first_both, first_pre, cotangent)
    parts = lax.all_to_all(grad, ALL, split_axis=0, concat_axis=0, tiled=True)
    mine = jnp.sum(parts, axis=0).astype(jnp.bfloat16)
    total = lax.all_to_all(
        jnp.broadcast_to(mine[None], (depth, 2, hidden)), ALL, split_axis=0, concat_axis=0, tiled=True
    )
    summed = jax.ShapeDtypeStruct((depth, hidden), jnp.float32)
    grad_self, grad_neigh = pl.pallas_call(
        finish_kernel,
        out_shape=(summed, summed),
        in_specs=[VMEM],
        out_specs=(VMEM, VMEM),
        compiler_params=PARAMS,
    )(total)
    return hidden_out, grad_self, grad_neigh


def solution(mesh):
    return jax.shard_map(
        per_device,
        mesh=mesh,
        in_specs=(
            P(ALL, None),
            P(),
            P(),
            P(ALL, None, None, None),
            P(ALL, None),
            P(ALL),
            P(ALL, None),
        ),
        out_specs=(P(ALL, None), P(), P()),
        check_vma=False,
    )
```

```python
import jax
import jax.numpy as jnp
from jax import lax
from jax.experimental import pallas as pl
from jax.experimental.pallas import tpu as pltpu
from jax.sharding import PartitionSpec as P

ALL = ("blk", "feat")
CONTRACT_FIRST = (((0,), (0,)), ((), ()))
CONTRACT_LAST = (((1,), (1,)), ((), ()))
RANGE = range(4)


def device(x, c, y, z):
    return (x * 2 + c) * 16 + y * 4 + z


PLANES = [[device(x, 0, y, z) for z in RANGE for x in RANGE] for y in RANGE]
PLANES += [[device(x, 1, y, z) for y in RANGE for x in RANGE] for z in RANGE]


def ring(step, to_other_core=0):
    pairs = []
    for x in RANGE:
        for y in RANGE:
            for z in RANGE:
                pairs.append((device(x, 0, y, z), device(x, to_other_core, (y + step) % 4, z)))
                pairs.append((device(x, 1, y, z), device(x, 1 - to_other_core, y, (z + step) % 4)))
    return pairs


RIGHT, LEFT, FAR = ring(1), ring(-1), ring(2)
RIGHT_ACROSS, LEFT_ACROSS, FAR_ACROSS = ring(1, 1), ring(-1, 1), ring(2, 1)
OTHER_CORE = [(d, d ^ 16) for d in range(128)]


def spread_kernel(in_ref, out_ref):
    copies, _, rows, size = out_ref.shape
    step = 16
    for k in range(in_ref.shape[1] // (step * size)):
        flat = in_ref[0:1, k * step * size : (k + 1) * step * size]
        block = flat.astype(jnp.float32).reshape(step, size).astype(jnp.bfloat16)
        x, first = divmod(k * step, rows)
        for copy in range(copies):
            out_ref[copy, x, first : first + step] = block


def turn_kernel(counts, tiles_ref, turned_ref):
    blocks, slots, size, _ = tiles_ref.shape
    for b in range(blocks):
        for t in range(slots):
            tile = tiles_ref[b, t]
            tile = jnp.where(t < counts[b], tile, jnp.zeros_like(tile))
            turned_ref[b, t * size : (t + 1) * size] = tile.T


def arrange_kernel(place, w_self_ref, w_neigh_ref, columns_ref, out_ref, columns_out_ref, wide_ref, placed_ref):
    columns_out_ref[...] = columns_ref[...]
    depth = w_self_ref.shape[0]
    wide_ref[:depth] = w_self_ref[...].astype(jnp.float32)
    wide_ref[depth:] = w_neigh_ref[...].astype(jnp.float32)
    for s, at, row in feature_rows(place):
        placed_ref[at : at + 1] = wide_ref[pl.ds(s * depth + row, 1)]
    out_ref[...] = placed_ref[...].astype(jnp.bfloat16)


def feature_rows(place):
    for k in range(8):
        first, stride = place[k], place[8 + k]
        for i in range(16):
            at = k // 4 * 128 + k % 4 * 16 + i
            row = first + (i % 4) * 32 + (i // 4) * stride
            yield 0, at, row
            yield 1, at + 64, row


def select_kernel(meta, lists, in_ref, w_ref, turned_ref, *refs):
    out_refs, rows_ref = refs[:-1], refs[-1]
    half = rows_ref.shape[0] // 2
    step = 16
    for part in range(2):
        first = ((meta[0] + part) % 2) * half
        for k in range(half // step):
            start = pl.multiple_of(first + k * step, step)
            rows_ref[pl.ds(part * half + k * step, step)] = jnp.swapaxes(
                in_ref[:, pl.ds(start, step), :], 0, 1
            )
    blocks, slots = lists.shape[2:]
    listed = blocks * slots
    for (place, part), out_ref in zip(MESSAGES, out_refs):
        for b in range(blocks):
            for t in range(slots):
                out_ref[b * slots + t] = rows_ref[part * half + lists[place, part, b, t]]
            out_ref[listed + b] = rows_ref[part * half + meta[1 + place] * blocks + b]


MESSAGES = ((2, 0), (1, 0), (0, 1), (3, 0), (3, 1), (2, 1), (1, 1), (0, 0))


def aggregate(pieces, turned_ref, both_ref):
    blocks, width, size = turned_ref.shape
    slots = width // size
    depth = both_ref.shape[0] // 2

    def features_of(k):
        return jnp.concatenate([piece[k] for piece in pieces], axis=0)

    for b in range(blocks):
        nodes = slice(b * size, (b + 1) * size)
        both_ref[:depth, nodes] = features_of(blocks * slots + b)
        x = jnp.concatenate([features_of(b * slots + t) for t in range(slots)], axis=1)
        gathered = jnp.dot(x, turned_ref[b], preferred_element_type=jnp.float32)
        both_ref[depth:, nodes] = gathered.astype(jnp.bfloat16)


def first_half_kernel(*refs):
    tiles_ref, w_ref, both_ref, pre_ref = refs[4:]
    aggregate(refs[:4], tiles_ref, both_ref)
    pre_ref[...] = lax.dot_general(
        both_ref[...], w_ref[:128], CONTRACT_FIRST, preferred_element_type=jnp.float32
    )


def second_half_kernel(place, *refs):
    tiles_ref, w_ref, first_ref, pre_ref, cot_ref, hidden_hbm, grad_ref, both_ref, hidden_ref, sems = refs[4:]
    aggregate(refs[:4], tiles_ref, both_ref)
    nodes = both_ref.shape[1]
    step = nodes // sems.shape[0]
    grad = jnp.zeros((2 * both_ref.shape[0], grad_ref.shape[2]), jnp.float32)
    stores = []
    for k in range(sems.shape[0]):
        rows = pl.ds(k * step, step)
        both = jnp.concatenate([first_ref[:, rows], both_ref[:, rows]], axis=0)
        pre = pre_ref[rows, :] + lax.dot_general(
            both_ref[:, rows], w_ref[128:], CONTRACT_FIRST, preferred_element_type=jnp.float32
        )
        s = jax.nn.sigmoid(pre)
        hidden = pre * s
        hidden_ref[rows, :] = hidden.astype(jnp.bfloat16)
        stores.append(pltpu.make_async_copy(hidden_ref.at[rows, :], hidden_hbm.at[rows, :], sems.at[k]))
        stores[-1].start()
        slope = s + hidden * (1.0 - s)
        grad_pre = (cot_ref[rows, :].astype(jnp.float32) * slope).astype(jnp.bfloat16)
        grad += jnp.dot(both, grad_pre, preferred_element_type=jnp.float32)
    for s, at, row in feature_rows(place):
        grad_ref[row, s : s + 1] = grad[at : at + 1]
    for store in stores:
        store.wait()


def finish_kernel(total_ref, grad_self_ref, grad_neigh_ref):
    grad_self_ref[...] = total_ref[:, 0, :].astype(jnp.float32)
    grad_neigh_ref[...] = total_ref[:, 1, :].astype(jnp.float32)


VMEM = pl.BlockSpec(memory_space=pltpu.VMEM)
SMEM = pl.BlockSpec(memory_space=pltpu.SMEM)
HBM = pl.BlockSpec(memory_space=pltpu.HBM)
ANY = pl.BlockSpec(memory_space=pl.ANY)
PARAMS = pltpu.CompilerParams(vmem_limit_bytes=24 * 1024 * 1024)


def send(array, pairs):
    return lax.ppermute(array, ALL, pairs)


def per_device(features, w_self, w_neigh, adjacency_tiles, tile_columns, tile_count, cotangent):
    depth, hidden = w_self.shape
    nodes = cotangent.shape[0]
    blocks, slots, size, _ = adjacency_tiles.shape
    core = lax.axis_index("blk") % 2
    feat = lax.axis_index("feat")
    y, z = feat // 4, feat % 4

    out = pl.pallas_call(
        spread_kernel,
        out_shape=jax.ShapeDtypeStruct((4, 4, 256, size), jnp.bfloat16),
        in_specs=[VMEM],
        out_specs=VMEM,
        compiler_params=PARAMS,
    )(features).reshape(16, 256, size)
    rows = lax.all_to_all(
        out, ALL, split_axis=0, concat_axis=0, tiled=True, axis_index_groups=PLANES
    )
    steps = jnp.array([0, 3, 1, 2], jnp.int32)
    ring_at = jnp.where(core == 0, y, z) + steps
    chip = jnp.where(core == 0, ring_at % 4 * 4 + z, y * 4 + ring_at % 4)
    meta = jnp.concatenate([core[None], chip]).astype(jnp.int32)
    piece_core = jnp.array([0, 0, 0, 1, 0, 1, 1, 1], jnp.int32) ^ core
    piece_at = jnp.where(piece_core == 0, y, z) + jnp.array([0, 3, 1, 3, 2, 2, 1, 0], jnp.int32)
    strides = jnp.where(piece_core == 0, 1, 4)
    first_rows = piece_core * 16 + piece_at % 4 * jnp.where(piece_core == 0, 4, 1)
    place = jnp.concatenate([first_rows, strides]).astype(jnp.int32)
    turned = pl.pallas_call(
        turn_kernel,
        out_shape=jax.ShapeDtypeStruct((blocks, slots * size, size), jnp.bfloat16),
        in_specs=[SMEM, VMEM],
        out_specs=VMEM,
        compiler_params=PARAMS,
    )(tile_count, adjacency_tiles)
    w, columns = pl.pallas_call(
        arrange_kernel,
        out_shape=(
            jax.ShapeDtypeStruct((2 * depth, hidden), jnp.bfloat16),
            jax.ShapeDtypeStruct(tile_columns.shape, tile_columns.dtype),
        ),
        in_specs=[SMEM, VMEM, VMEM, VMEM],
        out_specs=(VMEM, VMEM),
        scratch_shapes=[pltpu.VMEM((2 * depth, hidden), jnp.float32)] * 2,
        compiler_params=PARAMS,
    )(place, w_self, w_neigh, tile_columns)

    here = jnp.stack([columns, send(columns, OTHER_CORE)])
    lists = jnp.stack([here, send(here, RIGHT), send(here, LEFT), send(here, FAR)])
    listed = blocks * slots + blocks
    piece = jax.ShapeDtypeStruct((listed, 16, size), jnp.bfloat16)
    own_r, own_l, across, own_f, across_f, across_r, across_l, own = pl.pallas_call(
        select_kernel,
        out_shape=(piece,) * 8,
        in_specs=[SMEM, SMEM, VMEM, ANY, ANY],
        out_specs=(VMEM,) * 8,
        scratch_shapes=[pltpu.VMEM((256, 16, size), jnp.bfloat16)],
        compiler_params=PARAMS,
    )(meta, lists, rows, w, turned)
    first = [own, send(own_r, RIGHT)]
    first += [send(own_l, LEFT), send(across_r, RIGHT_ACROSS)]
    second = [send(own_f, FAR), send(across_f, FAR_ACROSS)]
    second += [send(across_l, LEFT_ACROSS), send(across, OTHER_CORE)]

    both = jax.ShapeDtypeStruct((depth, nodes), jnp.bfloat16)
    first_both, first_pre = pl.pallas_call(
        first_half_kernel,
        out_shape=(both, jax.ShapeDtypeStruct((nodes, hidden), jnp.float32)),
        in_specs=[VMEM] * 6,
        out_specs=(VMEM, VMEM),
        compiler_params=PARAMS,
    )(*first, turned, w)
    hidden_out, grad = pl.pallas_call(
        second_half_kernel,
        out_shape=(
            jax.ShapeDtypeStruct((nodes, hidden), jnp.bfloat16),
            jax.ShapeDtypeStruct((depth, 2, hidden), jnp.float32),
        ),
        in_specs=[SMEM] + [VMEM] * 9,
        out_specs=(ANY, VMEM),
        scratch_shapes=[
            pltpu.VMEM(both.shape, both.dtype),
            pltpu.VMEM((nodes, hidden), jnp.bfloat16),
            pltpu.SemaphoreType.DMA((2,)),
        ],
        compiler_params=PARAMS,
    )(place, *second, turned, w, first_both, first_pre, cotangent)
    parts = lax.all_to_all(grad, ALL, split_axis=0, concat_axis=0, tiled=True)
    mine = jnp.sum(parts, axis=0).astype(jnp.bfloat16)
    total = lax.all_to_all(
        jnp.broadcast_to(mine[None], (depth, 2, hidden)), ALL, split_axis=0, concat_axis=0, tiled=True
    )
    summed = jax.ShapeDtypeStruct((depth, hidden), jnp.float32)
    grad_self, grad_neigh = pl.pallas_call(
        finish_kernel,
        out_shape=(summed, summed),
        in_specs=[VMEM],
        out_specs=(VMEM, VMEM),
        compiler_params=PARAMS,
    )(total)
    return hidden_out, grad_self, grad_neigh


def solution(mesh):
    return jax.shard_map(
        per_device,
        mesh=mesh,
        in_specs=(
            P(ALL, None),
            P(),
            P(),
            P(ALL, None, None, None),
            P(ALL, None),
            P(ALL),
            P(ALL, None),
        ),
        out_specs=(P(ALL, None), P(), P()),
        check_vma=False,
    )
```

```python
import jax
import jax.numpy as jnp
from jax import lax
from jax.experimental import pallas as pl
from jax.experimental.pallas import tpu as pltpu
from jax.sharding import PartitionSpec as P

ALL = ("blk", "feat")
CONTRACT_FIRST = (((0,), (0,)), ((), ()))
CONTRACT_LAST = (((1,), (1,)), ((), ()))
RANGE = range(4)


def device(x, c, y, z):
    return (x * 2 + c) * 16 + y * 4 + z


PLANES = [[device(x, 0, y, z) for z in RANGE for x in RANGE] for y in RANGE]
PLANES += [[device(x, 1, y, z) for y in RANGE for x in RANGE] for z in RANGE]

EVERYONE = [[device(x, c, y, z) for y in RANGE for z in RANGE for x in RANGE for c in range(2)]]


def ring(step, to_other_core=0):
    pairs = []
    for x in RANGE:
        for y in RANGE:
            for z in RANGE:
                pairs.append((device(x, 0, y, z), device(x, to_other_core, (y + step) % 4, z)))
                pairs.append((device(x, 1, y, z), device(x, 1 - to_other_core, y, (z + step) % 4)))
    return pairs


RIGHT, LEFT, FAR = ring(1), ring(-1), ring(2)
RIGHT_ACROSS, LEFT_ACROSS, FAR_ACROSS = ring(1, 1), ring(-1, 1), ring(2, 1)
OTHER_CORE = [(d, d ^ 16) for d in range(128)]


def spread_kernel(in_ref, out_ref):
    copies, _, rows, size = out_ref.shape
    step = 16
    for k in range(in_ref.shape[1] // (step * size)):
        flat = in_ref[0:1, k * step * size : (k + 1) * step * size]
        block = flat.astype(jnp.float32).reshape(step, size).astype(jnp.bfloat16)
        x, first = divmod(k * step, rows)
        for copy in range(copies):
            out_ref[copy, x, first : first + step] = block


def turn_kernel(counts, tiles_ref, turned_ref):
    blocks, slots, size, _ = tiles_ref.shape
    for b in range(blocks):
        for t in range(slots):
            tile = tiles_ref[b, t]
            tile = jnp.where(t < counts[b], tile, jnp.zeros_like(tile))
            turned_ref[b, t * size : (t + 1) * size] = tile.T


def arrange_kernel(place, w_self_ref, w_neigh_ref, columns_ref, out_ref, columns_out_ref, wide_ref, placed_ref):
    columns_out_ref[...] = columns_ref[...]
    depth = w_self_ref.shape[0]
    wide_ref[:depth] = w_self_ref[...].astype(jnp.float32)
    wide_ref[depth:] = w_neigh_ref[...].astype(jnp.float32)
    for s, at, row in feature_rows(place):
        placed_ref[at : at + 1] = wide_ref[pl.ds(s * depth + row, 1)]
    out_ref[...] = placed_ref[...].astype(jnp.bfloat16)


def feature_rows(place):
    for k in range(8):
        first, stride = place[k], place[8 + k]
        for i in range(16):
            at = k // 4 * 128 + k % 4 * 16 + i
            row = first + (i % 4) * 32 + (i // 4) * stride
            yield 0, at, row
            yield 1, at + 64, row


def select_kernel(meta, lists, in_ref, w_ref, turned_ref, *refs):
    out_refs, rows_ref = refs[:-1], refs[-1]
    half = rows_ref.shape[0] // 2
    step = 16
    for part in range(2):
        first = ((meta[0] + part) % 2) * half
        for k in range(half // step):
            start = pl.multiple_of(first + k * step, step)
            rows_ref[pl.ds(part * half + k * step, step)] = jnp.swapaxes(
                in_ref[:, pl.ds(start, step), :], 0, 1
            )
    blocks, slots = lists.shape[2:]
    listed = blocks * slots
    for (place, part), out_ref in zip(MESSAGES, out_refs):
        for b in range(blocks):
            for t in range(slots):
                out_ref[b * slots + t] = rows_ref[part * half + lists[place, part, b, t]]
            out_ref[listed + b] = rows_ref[part * half + meta[1 + place] * blocks + b]


MESSAGES = ((2, 0), (1, 0), (0, 1), (3, 0), (3, 1), (2, 1), (1, 1), (0, 0))


def aggregate(pieces, turned_ref, both_ref):
    blocks, width, size = turned_ref.shape
    slots = width // size
    depth = both_ref.shape[0] // 2

    def features_of(k):
        return jnp.concatenate([piece[k] for piece in pieces], axis=0)

    for b in range(blocks):
        nodes = slice(b * size, (b + 1) * size)
        both_ref[:depth, nodes] = features_of(blocks * slots + b)
        x = jnp.concatenate([features_of(b * slots + t) for t in range(slots)], axis=1)
        gathered = jnp.dot(x, turned_ref[b], preferred_element_type=jnp.float32)
        both_ref[depth:, nodes] = gathered.astype(jnp.bfloat16)


def first_half_kernel(*refs):
    tiles_ref, w_ref, both_ref, pre_ref = refs[4:]
    aggregate(refs[:4], tiles_ref, both_ref)
    pre_ref[...] = lax.dot_general(
        both_ref[...], w_ref[:128], CONTRACT_FIRST, preferred_element_type=jnp.float32
    )


def second_half_kernel(place, *refs):
    tiles_ref, w_ref, first_ref, pre_ref, cot_ref, hidden_hbm, grad_ref, both_ref, hidden_ref, sems = refs[4:]
    aggregate(refs[:4], tiles_ref, both_ref)
    nodes = both_ref.shape[1]
    step = nodes // sems.shape[0]
    grad = jnp.zeros((2 * both_ref.shape[0], grad_ref.shape[2]), jnp.float32)
    stores = []
    for k in range(sems.shape[0]):
        rows = pl.ds(k * step, step)
        both = jnp.concatenate([first_ref[:, rows], both_ref[:, rows]], axis=0)
        pre = pre_ref[rows, :] + lax.dot_general(
            both_ref[:, rows], w_ref[128:], CONTRACT_FIRST, preferred_element_type=jnp.float32
        )
        s = jax.nn.sigmoid(pre)
        hidden = pre * s
        hidden_ref[rows, :] = hidden.astype(jnp.bfloat16)
        stores.append(pltpu.make_async_copy(hidden_ref.at[rows, :], hidden_hbm.at[rows, :], sems.at[k]))
        stores[-1].start()
        slope = s + hidden * (1.0 - s)
        grad_pre = (cot_ref[rows, :].astype(jnp.float32) * slope).astype(jnp.bfloat16)
        grad += jnp.dot(both, grad_pre, preferred_element_type=jnp.float32)
    for s, at, row in feature_rows(place):
        grad_ref[row, s : s + 1] = grad[at : at + 1]
    for store in stores:
        store.wait()


def finish_kernel(total_ref, grad_self_ref, grad_neigh_ref):
    grad_self_ref[...] = total_ref[:, 0, :].astype(jnp.float32)
    grad_neigh_ref[...] = total_ref[:, 1, :].astype(jnp.float32)


VMEM = pl.BlockSpec(memory_space=pltpu.VMEM)
SMEM = pl.BlockSpec(memory_space=pltpu.SMEM)
HBM = pl.BlockSpec(memory_space=pltpu.HBM)
ANY = pl.BlockSpec(memory_space=pl.ANY)
PARAMS = pltpu.CompilerParams(vmem_limit_bytes=24 * 1024 * 1024)


def send(array, pairs):
    return lax.ppermute(array, ALL, pairs)


def per_device(features, w_self, w_neigh, adjacency_tiles, tile_columns, tile_count, cotangent):
    depth, hidden = w_self.shape
    nodes = cotangent.shape[0]
    blocks, slots, size, _ = adjacency_tiles.shape
    core = lax.axis_index("blk") % 2
    feat = lax.axis_index("feat")
    y, z = feat // 4, feat % 4

    out = pl.pallas_call(
        spread_kernel,
        out_shape=jax.ShapeDtypeStruct((4, 4, 256, size), jnp.bfloat16),
        in_specs=[VMEM],
        out_specs=VMEM,
        compiler_params=PARAMS,
    )(features).reshape(16, 256, size)
    rows = lax.all_to_all(
        out, ALL, split_axis=0, concat_axis=0, tiled=True, axis_index_groups=PLANES
    )
    steps = jnp.array([0, 3, 1, 2], jnp.int32)
    ring_at = jnp.where(core == 0, y, z) + steps
    chip = jnp.where(core == 0, ring_at % 4 * 4 + z, y * 4 + ring_at % 4)
    meta = jnp.concatenate([core[None], chip]).astype(jnp.int32)
    piece_core = jnp.array([0, 0, 0, 1, 0, 1, 1, 1], jnp.int32) ^ core
    piece_at = jnp.where(piece_core == 0, y, z) + jnp.array([0, 3, 1, 3, 2, 2, 1, 0], jnp.int32)
    strides = jnp.where(piece_core == 0, 1, 4)
    first_rows = piece_core * 16 + piece_at % 4 * jnp.where(piece_core == 0, 4, 1)
    place = jnp.concatenate([first_rows, strides]).astype(jnp.int32)
    turned = pl.pallas_call(
        turn_kernel,
        out_shape=jax.ShapeDtypeStruct((blocks, slots * size, size), jnp.bfloat16),
        in_specs=[SMEM, VMEM],
        out_specs=VMEM,
        compiler_params=PARAMS,
    )(tile_count, adjacency_tiles)
    w, columns = pl.pallas_call(
        arrange_kernel,
        out_shape=(
            jax.ShapeDtypeStruct((2 * depth, hidden), jnp.bfloat16),
            jax.ShapeDtypeStruct(tile_columns.shape, tile_columns.dtype),
        ),
        in_specs=[SMEM, VMEM, VMEM, VMEM],
        out_specs=(VMEM, VMEM),
        scratch_shapes=[pltpu.VMEM((2 * depth, hidden), jnp.float32)] * 2,
        compiler_params=PARAMS,
    )(place, w_self, w_neigh, tile_columns)

    here = jnp.stack([columns, send(columns, OTHER_CORE)])
    lists = jnp.stack([here, send(here, RIGHT), send(here, LEFT), send(here, FAR)])
    listed = blocks * slots + blocks
    piece = jax.ShapeDtypeStruct((listed, 16, size), jnp.bfloat16)
    own_r, own_l, across, own_f, across_f, across_r, across_l, own = pl.pallas_call(
        select_kernel,
        out_shape=(piece,) * 8,
        in_specs=[SMEM, SMEM, VMEM, ANY, ANY],
        out_specs=(VMEM,) * 8,
        scratch_shapes=[pltpu.VMEM((256, 16, size), jnp.bfloat16)],
        compiler_params=PARAMS,
    )(meta, lists, rows, w, turned)
    first = [own, send(own_r, RIGHT)]
    first += [send(own_l, LEFT), send(across_r, RIGHT_ACROSS)]
    second = [send(own_f, FAR), send(across_f, FAR_ACROSS)]
    second += [send(across_l, LEFT_ACROSS), send(across, OTHER_CORE)]

    both = jax.ShapeDtypeStruct((depth, nodes), jnp.bfloat16)
    first_both, first_pre = pl.pallas_call(
        first_half_kernel,
        out_shape=(both, jax.ShapeDtypeStruct((nodes, hidden), jnp.float32)),
        in_specs=[VMEM] * 6,
        out_specs=(VMEM, VMEM),
        compiler_params=PARAMS,
    )(*first, turned, w)
    hidden_out, grad = pl.pallas_call(
        second_half_kernel,
        out_shape=(
            jax.ShapeDtypeStruct((nodes, hidden), jnp.bfloat16),
            jax.ShapeDtypeStruct((depth, 2, hidden), jnp.float32),
        ),
        in_specs=[SMEM] + [VMEM] * 9,
        out_specs=(ANY, VMEM),
        scratch_shapes=[
            pltpu.VMEM(both.shape, both.dtype),
            pltpu.VMEM((nodes, hidden), jnp.bfloat16),
            pltpu.SemaphoreType.DMA((2,)),
        ],
        compiler_params=PARAMS,
    )(place, *second, turned, w, first_both, first_pre, cotangent)
    parts = lax.all_to_all(
        grad, ALL, split_axis=0, concat_axis=0, tiled=True, axis_index_groups=EVERYONE
    )
    mine = jnp.sum(parts, axis=0).astype(jnp.bfloat16)
    total = lax.all_to_all(
        jnp.broadcast_to(mine[None], (depth, 2, hidden)), ALL, split_axis=0, concat_axis=0, tiled=True,
        axis_index_groups=EVERYONE,
    )
    summed = jax.ShapeDtypeStruct((depth, hidden), jnp.float32)
    grad_self, grad_neigh = pl.pallas_call(
        finish_kernel,
        out_shape=(summed, summed),
        in_specs=[VMEM],
        out_specs=(VMEM, VMEM),
        compiler_params=PARAMS,
    )(total)
    return hidden_out, grad_self, grad_neigh


def solution(mesh):
    return jax.shard_map(
        per_device,
        mesh=mesh,
        in_specs=(
            P(ALL, None),
            P(),
            P(),
            P(ALL, None, None, None),
            P(ALL, None),
            P(ALL),
            P(ALL, None),
        ),
        out_specs=(P(ALL, None), P(), P()),
        check_vma=False,
    )
```
